32 devices in a mesh: freq: 4 (over x, core), rcv: 8 (over z, y).
Axes of the slice: x: 2, y: 2, z: 4, core: 2. Of those that a mesh axis runs over, the one named last changes fastest.
Arguments:
- spectra: bfloat16 [2, 128, 384, 1024], P(None, None, 'freq', 'rcv'), may hold values from -600 to 600
- valid: int32 [384, 1024], P(None, 'rcv'), may hold values from 0 to 1, as said below
- sources: int32 [32], P('rcv'), may hold values from 0 to 1023, as said below
- bounds: int32 [32, 1024, 2], P('freq', 'rcv'), may hold values from 0 to 128, as said below
Outputs:
- lag_corr: bfloat16 [32, 1024, 128], P('freq', 'rcv')
- peak_value: float32 [32, 1024], P('freq', 'rcv')
The draws below stay inside these ranges and needn't reach their ends.
Inputs may be any that keep to these rules, and one draw needn't show every extreme that they name: `valid`: in each aligned group of 4 sub-windows at most one entry of a channel is 0. Source s is a channel from (s // 4) * 128 to (s // 4 + 1) * 128 - 1; the sources are distinct. bounds[s, c, 0] < bounds[s, c, 1] <= 128, and the window holds 16 to 64 lag samples.
All inputs are finite; a program needn't handle non-finite values.
Results may differ from the reference program's by a relative error of at most 0.007.
Values may be sent and summed in bfloat16 or wider, within the bound.
A program may use at most 128 MiB of HBM per device.

```python
import math
import jax
import jax.numpy as jnp
from jax import lax

F = 128
L = 128
W = 384
CH_DEV = 128
SRC_DEV = 4
S = 32
C = 1024


def draw_spectra(key, part):
    subkeys = jax.random.split(key, 3)
    row_scale = jnp.exp(jax.random.uniform(subkeys[0], (1, 1, W, C), minval=0.0, maxval=math.log(10.0)))
    bin_scale = jnp.exp(jax.random.uniform(subkeys[1], (1, F, 1, 1), minval=0.0, maxval=math.log(10.0)))
    values = jnp.clip(jax.random.normal(subkeys[2], (2, F, W, C), dtype=jnp.float32), -6.0, 6.0)
    return (values * row_scale * bin_scale).astype(jnp.bfloat16)


def draw_valid(key, part):
    dropped = jax.random.randint(key, (W // 4, 1, C), 0, 5)
    within = jnp.arange(4, dtype=jnp.int32)[None, :, None]
    return (within != dropped).astype(jnp.int32).reshape(W, C)


def draw_sources(key, part):
    blocks = S // SRC_DEV
    scores = jax.random.randint(key, (blocks, CH_DEV), 0, 2 ** 20) * CH_DEV + jnp.arange(CH_DEV, dtype=jnp.int32)[None, :]
    scores = scores.at[0, 0].set(-2)
    scores = scores.at[blocks - 1, CH_DEV - 1].set(-1)
    chosen = jnp.argsort(scores, axis=1)[:, :SRC_DEV].astype(jnp.int32)
    offsets = jnp.arange(blocks, dtype=jnp.int32)[:, None] * CH_DEV
    return (offsets + chosen).reshape(S).astype(jnp.int32)


def draw_bounds(key, part):
    subkeys = jax.random.split(key, 2)
    widths = jax.random.randint(subkeys[0], (S, C, 1), L // 8, L // 2 + 1)
    lower = jax.random.randint(subkeys[1], (S, C, 1), 0, L - widths + 1)
    return jnp.concatenate([lower, lower + widths], axis=2).astype(jnp.int32)


def setup_inputs(seed: int = 0) -> dict:
    keys = jax.random.split(jax.random.key(seed), 5)
    spectra = draw_spectra(jax.random.fold_in(keys[4], 71), 0)
    valid = draw_valid(jax.random.fold_in(keys[4], 71), 0)
    sources = draw_sources(jax.random.fold_in(keys[4], 71), 0)
    bounds = draw_bounds(jax.random.fold_in(keys[4], 71), 0)
    return {"spectra": spectra, "valid": valid, "sources": sources, "bounds": bounds}


def whiten(block, valid_block):
    spectra_f = block.astype(jnp.float32)
    energy = lax.optimization_barrier(jnp.mean(spectra_f[0] * spectra_f[0] + spectra_f[1] * spectra_f[1], axis=0))
    scaling = valid_block.astype(jnp.float32) / jnp.sqrt(energy + 1e-06)
    return (spectra_f * scaling).astype(jnp.bfloat16)

def make_tables(bin_first, bin_count, lag_count, period):
    bins_col = (bin_first + 1 + jnp.arange(bin_count, dtype=jnp.int32))[:, None]
    lag_row = jnp.arange(lag_count, dtype=jnp.int32)[None, :] - lag_count // 2
    phase_int = bins_col * lag_row % period
    angles = phase_int.astype(jnp.float32) * (2.0 * math.pi / period)
    return (jnp.cos(angles).astype(jnp.bfloat16), jnp.sin(angles).astype(jnp.bfloat16))

def reference(spectra, valid, sources, bounds):
    source_white = whiten(spectra[:, :, :, sources], valid[:, sources]).astype(jnp.float32)
    source_valid = valid[:, sources].astype(jnp.float32)
    cos_table, sin_table = make_tables(0, F, L, 2 * F)
    cos_f = cos_table.astype(jnp.float32)
    sin_f = sin_table.astype(jnp.float32)
    blocks = S // SRC_DEV

    def one_block(block_id):
        first = (block_id * CH_DEV).astype(jnp.int32)
        white_block = whiten(lax.dynamic_slice_in_dim(spectra, first, CH_DEV, 3), lax.dynamic_slice_in_dim(valid, first, CH_DEV, 1)).astype(jnp.float32)
        valid_block = lax.dynamic_slice_in_dim(valid, first, CH_DEV, 1).astype(jnp.float32)
        bound_block = lax.dynamic_slice_in_dim(bounds, first, CH_DEV, 1)
        cross_re = jnp.einsum('fws,fwc->fsc', source_white[0], white_block[0]) + jnp.einsum('fws,fwc->fsc', source_white[1], white_block[1])
        cross_im = jnp.einsum('fws,fwc->fsc', source_white[0], white_block[1]) - jnp.einsum('fws,fwc->fsc', source_white[1], white_block[0])
        pair_count = jnp.dot(source_valid.T, valid_block, preferred_element_type=jnp.float32)
        stack_re = (cross_re / pair_count).astype(jnp.bfloat16).astype(jnp.float32)
        stack_im = (cross_im / pair_count).astype(jnp.bfloat16).astype(jnp.float32)
        lag_corr = (jnp.einsum('fsc,ft->sct', stack_re, cos_f) - jnp.einsum('fsc,ft->sct', stack_im, sin_f)).astype(jnp.bfloat16)
        lag_index = jnp.arange(L, dtype=jnp.int32)[None, None, :]
        inside = (lag_index >= bound_block[:, :, 0:1]) & (lag_index < bound_block[:, :, 1:2])
        peak_value = lax.optimization_barrier(jnp.max(jnp.where(inside, lag_corr.astype(jnp.float32), -jnp.inf), axis=2))
        return (lag_corr, peak_value)
    corr_blocks, peak_blocks = lax.map(one_block, jnp.arange(blocks, dtype=jnp.int32))
    lag_corr = jnp.moveaxis(corr_blocks, 0, 1).reshape(S, C, L)
    peak_value = jnp.moveaxis(peak_blocks, 0, 1).reshape(S, C)
    return (lag_corr, peak_value)
```

```python
import math

import jax
import jax.numpy as jnp
from jax import lax
from jax.sharding import PartitionSpec as P

L = 128


def make_tables(bin_count, lag_count, period):
    bins_col = (1 + jnp.arange(bin_count, dtype=jnp.int32))[:, None]
    lag_row = jnp.arange(lag_count, dtype=jnp.int32)[None, :] - lag_count // 2
    phase_int = bins_col * lag_row % period
    angles = phase_int.astype(jnp.float32) * (2.0 * math.pi / period)
    return (jnp.cos(angles).astype(jnp.bfloat16), jnp.sin(angles).astype(jnp.bfloat16))


def local(spectra, valid, sources, bounds):
    freq_index = lax.axis_index("freq")
    rcv_index = lax.axis_index("rcv")
    window_rows = spectra.shape[2]
    channels = valid.shape[1]
    bins = spectra.shape[1]
    own_valid = lax.dynamic_slice_in_dim(valid, freq_index * window_rows, window_rows, 0).astype(
        jnp.float32
    )
    spectra_f = spectra.astype(jnp.float32)
    energy = jnp.mean(spectra_f[0] * spectra_f[0] + spectra_f[1] * spectra_f[1], axis=0)
    scaling = own_valid / jnp.sqrt(energy + 1e-06)
    whitened = (spectra_f * scaling).astype(jnp.bfloat16)
    offsets = sources - rcv_index * channels
    onehot = (offsets[:, None] == jnp.arange(channels, dtype=jnp.int32)[None, :]).astype(jnp.bfloat16)
    valid_half = valid.astype(jnp.bfloat16)
    picked = jnp.einsum("pfwc,sc->fspw", whitened, onehot)
    picked_valid = jnp.einsum("wc,sc->sw", valid_half, onehot)
    source_part = lax.all_gather(picked, "rcv", axis=1, tiled=True)
    source_valid = lax.all_gather(picked_valid, "rcv", axis=0, tiled=True)
    swapped = jnp.stack([whitened[1], -whitened[0]], axis=0)
    part_re = jnp.einsum("fspw,pfwc->fsc", source_part, whitened, preferred_element_type=jnp.float32)
    part_im = jnp.einsum("fspw,pfwc->fsc", source_part, swapped, preferred_element_type=jnp.float32)
    counts = jnp.einsum("sw,wc->sc", source_valid, valid_half, preferred_element_type=jnp.float32)
    stack_re = (part_re / counts).astype(jnp.bfloat16)
    stack_im = (part_im / counts).astype(jnp.bfloat16)
    full_cos, full_sin = make_tables(bins, L, 2 * bins)
    partial = jnp.einsum(
        "fsc,ft->sct", stack_re, full_cos, preferred_element_type=jnp.float32
    ) - jnp.einsum("fsc,ft->sct", stack_im, full_sin, preferred_element_type=jnp.float32)
    lag_sum = lax.psum_scatter(partial, "freq", scatter_dimension=0, tiled=True)
    lag_corr = lag_sum.astype(jnp.bfloat16)
    lag_index = jnp.arange(L, dtype=jnp.int32)[None, None, :]
    inside = (lag_index >= bounds[:, :, 0:1]) & (lag_index < bounds[:, :, 1:2])
    peak_value = jnp.max(jnp.where(inside, lag_corr.astype(jnp.float32), -jnp.inf), axis=2)
    return (lag_corr, peak_value)


def solution(mesh):
    in_specs = (P(None, None, "freq", "rcv"), P(None, "rcv"), P("rcv"), P("freq", "rcv", None))
    out_specs = (P("freq", "rcv", None), P("freq", "rcv"))
    return jax.shard_map(local, mesh=mesh, in_specs=in_specs, out_specs=out_specs, check_vma=False)
```

```python
import functools
import math

import jax
import jax.numpy as jnp
import numpy as np
from jax import lax
from jax.experimental import pallas as pl
from jax.experimental.pallas import tpu as pltpu
from jax.sharding import PartitionSpec as P

L = 128
CHUNKS = 4
MESH = pl.DeviceIdType.MESH
BF = jnp.bfloat16
F32 = jnp.float32
NT = (((1,), (1,)), ((), ()))


def lag_table(bins, per, lags):
    phase = (np.arange(1, bins + 1)[:, None] * (np.arange(lags) - lags // 2)[None, :]) % (2 * bins)
    angle = phase.astype(np.float32) * np.float32(2.0 * math.pi / (2 * bins))
    both = np.stack([np.cos(angle), -np.sin(angle)]).astype(BF).astype(np.float32)
    table = np.einsum("pft,su->stpfu", both, np.eye(per, dtype=np.float32))
    return table.reshape(per * lags, 2 * bins * per).astype(BF)


def kernel(n, sources_ref, low_ref, high_ref, spectra_ref, valid_ref, table_ref, lag_ref, peak_ref,
           white, own_valid, table, picks, cross, part, from_core, from_x, to_x,
           load_sem, valid_sem, table_sem, send_sem, near_sem, pass_sem, recv_sem, red_send, red_recv):
    _, bins, rows, chans = white.shape
    per = sources_ref.shape[0]
    half = n // 2
    step = bins // CHUNKS
    group = n // 4
    fi = lax.axis_index("freq")
    r = lax.axis_index("rcv")
    x_idx, core = fi // 2, lax.rem(fi, 2)
    near = r + 1 - 2 * lax.rem(r, 2)
    peers = [lax.rem(r + 2 * d, n) for d in range(1, half)]
    core_dev = fi + 1 - 2 * core
    x_dev = lax.rem(fi + 2, 4)

    barrier = pltpu.get_barrier_semaphore()
    for dev in [(fi, near)] + [(fi, p) for p in peers] + [(core_dev, r), (x_dev, r)]:
        pl.semaphore_signal(barrier, inc=1, device_id=dev, device_id_type=MESH)

    def load(k):
        part_f = pl.ds(k * step, step)
        return pltpu.make_async_copy(spectra_ref.at[:, part_f], white.at[:, part_f], load_sem.at[k])

    for k in range(CHUNKS):
        load(k).start()
    valid_copy = pltpu.make_async_copy(valid_ref.at[pl.ds(fi * rows, rows)], own_valid, valid_sem)
    valid_copy.start()
    table_copy = pltpu.make_async_copy(table_ref, table, table_sem)
    table_copy.start()

    total = jnp.zeros((rows, chans), F32)
    for k in range(CHUNKS):
        load(k).wait()

        def add(i, acc, k=k):
            for u in range(4):
                f = k * step + i * 4 + u
                a = white[0, f].astype(F32)
                b = white[1, f].astype(F32)
                acc = acc + (a * a + b * b)
            return acc

        total = lax.fori_loop(0, step // 4, add, total)
    valid_copy.wait()
    valid_f = own_valid[...].astype(F32)
    scale = valid_f / jnp.sqrt(total * (1.0 / bins) + 1e-6)
    valid_w = jnp.concatenate([valid_f, jnp.zeros((chans - rows, chans), F32)], axis=0).astype(BF)

    row_id = lax.broadcasted_iota(jnp.int32, (4 * per, chans), 0)
    lane_id = lax.broadcasted_iota(jnp.int32, (4 * per, chans), 1)
    hit = jnp.zeros((4 * per, chans), F32)
    for s in range(per):
        off = sources_ref[s] - r * chans
        hit = jnp.where((lax.rem(row_id, per) == s) & (lane_id == off), 1.0, hit)
    pick = jnp.concatenate(
        [jnp.where(row_id // per == u, hit, 0.0) for u in range(4)], axis=1).astype(BF)
    tile = 4 * per
    picks[r, 0:tile] = lax.dot_general(
        hit.astype(BF), valid_w, NT, preferred_element_type=F32).astype(BF)

    pairs = step // 8
    width = 3 * tile * pairs

    def span(k):
        return pl.ds(0, tile + width) if k == 0 else pl.ds(tile + k * width, width)

    def send(block, k, to, sem):
        return pltpu.make_async_remote_copy(
            src_ref=picks.at[block, span(k)], dst_ref=picks.at[block, span(k)],
            send_sem=sem, recv_sem=recv_sem.at[block, k],
            device_id=(fi, to), device_id_type=MESH)

    def forward(k):
        for d, p in enumerate(peers):
            send(p, k, near, pass_sem.at[d, k]).wait_recv()
            send(p, k, near, pass_sem.at[d, k]).start()

    rest = chans - rows
    for k in range(CHUNKS):
        def whiten(i, _, k=k):
            top, low = [], []
            for u in range(8):
                f = k * step + i * 8 + u
                re = (white[0, f].astype(F32) * scale).astype(BF)
                im = (white[1, f].astype(F32) * scale).astype(BF)
                white[0, f] = re
                white[1, f] = im
                top.append(jnp.concatenate([re, im[0:rest]], axis=0))
                low.append(im[rest:])
            first = jnp.concatenate(top[0:4], axis=1)
            second = jnp.concatenate(top[4:8], axis=1)
            third = jnp.concatenate(
                [jnp.concatenate(low[0:4], axis=1), jnp.concatenate(low[4:8], axis=1)], axis=0)
            base = pl.multiple_of(tile + k * width + i * (3 * tile), tile)
            for m, w in enumerate((first, second, third)):
                picks[r, pl.ds(base + m * tile, tile)] = lax.dot_general(
                    pick, w, NT, preferred_element_type=F32).astype(BF)
            return 0

        lax.fori_loop(0, pairs, whiten, 0)
        if k == 0:
            pl.semaphore_wait(barrier, half + 2)
        send(r, k, near, near_sem.at[k]).start()
        for d, p in enumerate(peers):
            send(r, k, p, send_sem.at[d, k]).start()
        if k >= 1:
            forward(k - 1)

    forward(CHUNKS - 1)
    band = lax.broadcasted_iota(jnp.int32, (n, tile, chans), 1) // per
    blank = jnp.zeros((2 * chans - 2 * rows, chans), BF)
    for k in range(CHUNKS):
        send(near, k, near, near_sem.at[k]).wait_recv()
        for p in peers:
            other = p + 1 - 2 * lax.rem(p, 2)
            send(other, k, near, near_sem.at[k]).wait_recv()

        def correlate(i, _, k=k):
            base = pl.multiple_of(tile + k * width + i * (3 * tile), tile)
            shared = picks[:, pl.ds(base + 2 * tile, tile)].reshape(n * tile, chans)
            for q in range(2):
                lead = picks[:, pl.ds(base + q * tile, tile)].reshape(n * tile, chans)
                lhs = jnp.concatenate([lead, shared], axis=1)
                out_re = out_im = None
                for u in range(4):
                    f = k * step + i * 8 + q * 4 + u
                    re = white[0, f]
                    im = white[1, f]
                    neg = -re
                    if q == 0:
                        left = jnp.concatenate([re, im, blank], axis=0)
                        right = jnp.concatenate([im, neg, blank], axis=0)
                    else:
                        left = jnp.concatenate([re, im[0:rest], blank, im[rest:]], axis=0)
                        right = jnp.concatenate([im, neg[0:rest], blank, neg[rest:]], axis=0)
                    out = jnp.dot(lhs, jnp.concatenate([left, right], axis=1),
                                  preferred_element_type=F32)
                    one = out[:, 0:chans].reshape(n, tile, chans)
                    two = out[:, chans:].reshape(n, tile, chans)
                    out_re = one if u == 0 else jnp.where(band == u, one, out_re)
                    out_im = two if u == 0 else jnp.where(band == u, two, out_im)
                at = pl.multiple_of((k * step + i * 8 + q * 4) * per, tile)
                cross[:, pl.ds(at, tile)] = out_re.astype(BF)
                cross[:, pl.ds(bins * per + at, tile)] = out_im.astype(BF)
            return 0

        lax.fori_loop(0, pairs, correlate, 0)

    counts = jnp.dot(picks[:, 0:tile].reshape(n * tile, chans), valid_w, preferred_element_type=F32)
    body = per * L
    part[:, body:body + tile] = counts.reshape(n, tile, chans).astype(BF)
    table_copy.wait()

    def transform(i):
        def one(j, _):
            at = i * group + j
            part[at, 0:body] = jnp.dot(
                table[...], cross[at], preferred_element_type=F32).astype(BF)
            return 0

        lax.fori_loop(0, group, one, 0)

    def to_core(i, slot):
        return pltpu.make_async_remote_copy(
            src_ref=part.at[pl.ds(i * group, group)], dst_ref=from_core.at[slot],
            send_sem=red_send.at[slot], recv_sem=red_recv.at[slot],
            device_id=(core_dev, r), device_id_type=MESH)

    far_other = 2 * (1 - x_idx) + (1 - core)
    far_same = 2 * (1 - x_idx) + core
    transform(far_other)
    to_core(far_other, 0).start()
    transform(far_same)
    to_core(far_other, 0).wait_recv()

    def join(j, _):
        to_x[j] = (part[far_same * group + j].astype(F32) + from_core[0, j].astype(F32)).astype(BF)
        return 0

    lax.fori_loop(0, group, join, 0)
    cross_x = pltpu.make_async_remote_copy(
        src_ref=to_x, dst_ref=from_x, send_sem=red_send.at[2], recv_sem=red_recv.at[2],
        device_id=(x_dev, r), device_id_type=MESH)
    cross_x.start()
    transform(core_dev)
    to_core(core_dev, 1).start()
    transform(fi)
    to_core(core_dev, 1).wait_recv()
    cross_x.wait_recv()

    lag_id = lax.broadcasted_iota(jnp.int32, (L, chans), 0)

    def finish(j, _):
        def added(a, b):
            return (part[fi * group + j, a:b].astype(F32) + from_core[1, j, a:b].astype(F32)
                    + from_x[j, a:b].astype(F32))

        count = added(body, body + tile)
        for s in range(per):
            lag = added(s * L, s * L + L) / count[s:s + 1]
            lag = lag.astype(BF).astype(F32)
            row = j * per + s
            low = low_ref[pl.ds(row, 1), :]
            high = high_ref[pl.ds(row, 1), :]
            inside = (lag_id >= low) & (lag_id < high)
            peak_ref[pl.ds(row, 1), :] = jnp.max(
                jnp.where(inside, lag, -jnp.inf), axis=0, keepdims=True)
            lag_ref[row] = lag.T.astype(BF)
        return 0

    lax.fori_loop(0, group, finish, 0)

    for k in range(CHUNKS):
        send(r, k, near, near_sem.at[k]).wait_send()
        for d, p in enumerate(peers):
            send(r, k, p, send_sem.at[d, k]).wait_send()
            send(p, k, near, pass_sem.at[d, k]).wait_send()
    to_core(far_other, 0).wait_send()
    to_core(core_dev, 1).wait_send()
    cross_x.wait_send()


def local(n, spectra, valid, sources, bounds):
    _, bins, rows, chans = spectra.shape
    per = sources.shape[0]
    group = n // 4
    count = bounds.shape[0]
    table = jnp.asarray(lag_table(bins, per, L))
    span = per * L + 4 * per
    vmem = pl.BlockSpec(memory_space=pltpu.VMEM)
    hbm = pl.BlockSpec(memory_space=pl.ANY)
    dma = pltpu.SemaphoreType.DMA
    half = n // 2
    return pl.pallas_call(
        functools.partial(kernel, n),
        out_shape=(jax.ShapeDtypeStruct((count, chans, L), BF),
                   jax.ShapeDtypeStruct((count, chans), F32)),
        in_specs=[pl.BlockSpec(memory_space=pltpu.SMEM), vmem, vmem, hbm, hbm, hbm],
        out_specs=(vmem, vmem),
        scratch_shapes=[
            pltpu.VMEM((2, bins, rows, chans), BF),
            pltpu.VMEM((rows, chans), jnp.int32),
            pltpu.VMEM(table.shape, BF),
            pltpu.VMEM((n, 4 * per + bins // 8 * 12 * per, chans), BF),
            pltpu.VMEM((n, 2 * bins * per, chans), BF),
            pltpu.VMEM((n, span, chans), BF),
            pltpu.VMEM((2, group, span, chans), BF),
            pltpu.VMEM((group, span, chans), BF),
            pltpu.VMEM((group, span, chans), BF),
            dma((CHUNKS,)), dma, dma,
            dma((half, CHUNKS)), dma((CHUNKS,)), dma((half, CHUNKS)), dma((n, CHUNKS)),
            dma((3,)), dma((3,)),
        ],
        compiler_params=pltpu.CompilerParams(
            collective_id=0, has_side_effects=True, vmem_limit_bytes=60 * 1024 * 1024),
    )(sources, bounds[:, :, 0], bounds[:, :, 1], spectra, valid, table)


def solution(mesh):
    in_specs = (P(None, None, "freq", "rcv"), P(None, "rcv"), P("rcv"), P("freq", "rcv", None))
    out_specs = (P("freq", "rcv", None), P("freq", "rcv"))
    return jax.shard_map(functools.partial(local, mesh.shape["rcv"]), mesh=mesh,
                         in_specs=in_specs, out_specs=out_specs, check_vma=False)
```

```python
import functools
import math

import jax
import jax.numpy as jnp
import numpy as np
from jax import lax
from jax.experimental import pallas as pl
from jax.experimental.pallas import tpu as pltpu
from jax.sharding import PartitionSpec as P

L = 128
CHUNKS = 8
EARLY = 2
MESH = pl.DeviceIdType.MESH
BF = jnp.bfloat16
F32 = jnp.float32
NT = (((1,), (1,)), ((), ()))


def lag_table(bins, per, lags):
    phase = (np.arange(1, bins + 1)[:, None] * (np.arange(lags) - lags // 2)[None, :]) % (2 * bins)
    angle = phase.astype(np.float32) * np.float32(2.0 * math.pi / (2 * bins))
    both = np.stack([np.cos(angle), -np.sin(angle)]).astype(BF).astype(np.float32)
    table = np.einsum("pft,su->stpfu", both, np.eye(per, dtype=np.float32))
    return table.reshape(per * lags, 2 * bins * per).astype(BF)


def kernel(n, sources_ref, spectra_ref, valid_ref, table_ref, total_ref,
           white, own_valid, table, picks, scales, cross, part, from_core, from_x, to_x,
           load_sem, valid_sem, table_sem, send_sem, near_sem, pass_sem, recv_sem, red_send, red_recv):
    _, bins, rows, chans = white.shape
    per = sources_ref.shape[0]
    half = n // 2
    step = bins // CHUNKS
    group = n // 4
    piece = group // 2
    fi = lax.axis_index("freq")
    r = lax.axis_index("rcv")
    x_idx, core = fi // 2, lax.rem(fi, 2)
    near = r + 1 - 2 * lax.rem(r, 2)
    peers = [lax.rem(r + 2 * d, n) for d in range(1, half)]
    core_dev = fi + 1 - 2 * core
    x_dev = lax.rem(fi + 2, 4)

    barrier = pltpu.get_barrier_semaphore()
    for dev in [(fi, near)] + [(fi, p) for p in peers] + [(core_dev, r), (x_dev, r)]:
        pl.semaphore_signal(barrier, inc=1, device_id=dev, device_id_type=MESH)

    def load(k):
        part_f = pl.ds(k * step, step)
        return pltpu.make_async_copy(spectra_ref.at[:, part_f], white.at[:, part_f], load_sem.at[k])

    for k in range(CHUNKS):
        load(k).start()
    valid_copy = pltpu.make_async_copy(valid_ref.at[pl.ds(fi * rows, rows)], own_valid, valid_sem)
    valid_copy.start()
    table_copy = pltpu.make_async_copy(table_ref, table, table_sem)
    table_copy.start()

    row_id = lax.broadcasted_iota(jnp.int32, (4 * per, chans), 0)
    lane_id = lax.broadcasted_iota(jnp.int32, (4 * per, chans), 1)
    hit = jnp.zeros((4 * per, chans), F32)
    for s in range(per):
        off = sources_ref[s] - r * chans
        hit = jnp.where((lax.rem(row_id, per) == s) & (lane_id == off), 1.0, hit)
    pick = jnp.concatenate(
        [jnp.where(row_id // per == u, hit, 0.0) for u in range(4)], axis=1).astype(BF)
    hit = hit.astype(BF)
    tile = 4 * per
    pairs = step // 8
    width = 3 * tile * pairs
    rest = chans - rows

    def send(block, k, to, sem):
        ref = scales.at[block] if k == CHUNKS else picks.at[block, pl.ds(k * width, width)]
        return pltpu.make_async_remote_copy(
            src_ref=ref, dst_ref=ref, send_sem=sem, recv_sem=recv_sem.at[block, k],
            device_id=(fi, to), device_id_type=MESH)

    def send_own(k):
        send(r, k, near, near_sem.at[k]).start()
        for d, p in enumerate(peers):
            send(r, k, p, send_sem.at[d, k]).start()

    def forward(k):
        for d, p in enumerate(peers):
            send(p, k, near, pass_sem.at[d, k]).wait_recv()
            send(p, k, near, pass_sem.at[d, k]).start()

    def arrive(k):
        send(near, k, near, near_sem.at[k]).wait_recv()
        for p in peers:
            other = p + 1 - 2 * lax.rem(p, 2)
            send(other, k, near, near_sem.at[k]).wait_recv()

    def choose(k):
        def one(i, _):
            top, low = [], []
            for u in range(8):
                f = k * step + i * 8 + u
                im = white[1, f]
                top.append(jnp.concatenate([white[0, f], im[0:rest]], axis=0))
                low.append(im[rest:])
            first = jnp.concatenate(top[0:4], axis=1)
            second = jnp.concatenate(top[4:8], axis=1)
            third = jnp.concatenate(
                [jnp.concatenate(low[0:4], axis=1), jnp.concatenate(low[4:8], axis=1)], axis=0)
            base = pl.multiple_of(k * width + i * (3 * tile), tile)
            for m, w in enumerate((first, second, third)):
                picks[r, pl.ds(base + m * tile, tile)] = lax.dot_general(
                    pick, w, NT, preferred_element_type=F32).astype(BF)
            return 0

        lax.fori_loop(0, pairs, one, 0)

    for k in range(EARLY):
        load(k).wait()
        choose(k)
        if k == 0:
            pl.semaphore_wait(barrier, half + 2)
        send_own(k)

    total = jnp.zeros((rows, chans), F32)
    for k in range(CHUNKS):
        if k >= EARLY:
            load(k).wait()

        def add(i, acc, k=k):
            for u in range(4):
                f = k * step + i * 4 + u
                a = white[0, f].astype(F32)
                b = white[1, f].astype(F32)
                acc = acc + (a * a + b * b)
            return acc

        total = lax.fori_loop(0, step // 4, add, total)
    valid_copy.wait()
    valid_f = own_valid[...].astype(F32)
    scale = valid_f / jnp.sqrt(total * (1.0 / bins) + 1e-6)
    valid_w = jnp.concatenate([valid_f, jnp.zeros((chans - rows, chans), F32)], axis=0).astype(BF)
    left_over = jnp.concatenate([scale, scale[0:rest], scale[rest:], scale[rest:]], axis=0)
    chosen = jnp.zeros((tile, 2 * chans), F32)
    for _ in range(3):
        high = left_over.astype(BF)
        left_over = left_over - high.astype(F32)
        chosen = chosen + lax.dot_general(hit, high, NT, preferred_element_type=F32)
    scales[r] = chosen
    send_own(CHUNKS)

    for k in range(EARLY, CHUNKS):
        choose(k)
        send_own(k)
        forward(k - EARLY)
        if k == EARLY:
            forward(CHUNKS)

    band = lax.broadcasted_iota(jnp.int32, (n, tile, chans), 1) // per
    blank = jnp.zeros((2 * chans - 2 * rows, chans), BF)

    def correlate(k):
        def one(i, _):
            base = pl.multiple_of(k * width + i * (3 * tile), tile)

            def sources_of(m, lanes):
                raw = picks[:, pl.ds(base + m * tile, tile)].astype(F32)
                return (raw * scales[:, :, lanes]).astype(BF).reshape(n * tile, chans)

            shared = sources_of(2, slice(chans, 2 * chans))
            for q in range(2):
                lhs = jnp.concatenate([sources_of(q, slice(0, chans)), shared], axis=1)
                out_re = out_im = None
                for u in range(4):
                    f = k * step + i * 8 + q * 4 + u
                    re = (white[0, f].astype(F32) * scale).astype(BF)
                    im = (white[1, f].astype(F32) * scale).astype(BF)
                    neg = -re
                    if q == 0:
                        left = jnp.concatenate([re, im, blank], axis=0)
                        right = jnp.concatenate([im, neg, blank], axis=0)
                    else:
                        left = jnp.concatenate([re, im[0:rest], blank, im[rest:]], axis=0)
                        right = jnp.concatenate([im, neg[0:rest], blank, neg[rest:]], axis=0)
                    out = jnp.dot(lhs, jnp.concatenate([left, right], axis=1),
                                  preferred_element_type=F32)
                    first = out[:, 0:chans].reshape(n, tile, chans)
                    second = out[:, chans:].reshape(n, tile, chans)
                    out_re = first if u == 0 else jnp.where(band == u, first, out_re)
                    out_im = second if u == 0 else jnp.where(band == u, second, out_im)
                at = pl.multiple_of((k * step + i * 8 + q * 4) * per, tile)
                cross[:, pl.ds(at, tile)] = out_re.astype(BF)
                cross[:, pl.ds(bins * per + at, tile)] = out_im.astype(BF)
            return 0

        lax.fori_loop(0, pairs, one, 0)

    body = per * L
    for k in range(CHUNKS):
        if k + CHUNKS - EARLY < CHUNKS:
            forward(k + CHUNKS - EARLY)
        if k == 0:
            arrive(CHUNKS)
            usable = jnp.where(scales[:, :, 0:chans] > 0.0, 1.0, 0.0)
            counts = jnp.dot(usable.astype(BF).reshape(n * tile, chans), valid_w,
                             preferred_element_type=F32)
            part[:, body:body + tile] = counts.reshape(n, tile, chans).astype(BF)
        arrive(k)
        correlate(k)
    table_copy.wait()

    def transform(i, h):
        def one(j, _):
            at = i * group + h * piece + j
            part[at, 0:body] = jnp.dot(
                table[...], cross[at], preferred_element_type=F32).astype(BF)
            return 0

        lax.fori_loop(0, piece, one, 0)

    def to_core(i, slot, h):
        return pltpu.make_async_remote_copy(
            src_ref=part.at[pl.ds(i * group + h * piece, piece)],
            dst_ref=from_core.at[slot, pl.ds(h * piece, piece)],
            send_sem=red_send.at[slot, h], recv_sem=red_recv.at[slot, h],
            device_id=(core_dev, r), device_id_type=MESH)

    def over_x(h):
        mine = pl.ds(h * piece, piece)
        return pltpu.make_async_remote_copy(
            src_ref=to_x.at[mine], dst_ref=from_x.at[mine],
            send_sem=red_send.at[2, h], recv_sem=red_recv.at[2, h],
            device_id=(x_dev, r), device_id_type=MESH)

    far_other = 2 * (1 - x_idx) + (1 - core)
    far_same = 2 * (1 - x_idx) + core
    for h in range(2):
        transform(far_other, h)
        to_core(far_other, 0, h).start()
    for h in range(2):
        transform(far_same, h)
        to_core(far_other, 0, h).wait_recv()

        def join(j, _, h=h):
            at = h * piece + j
            to_x[at] = (part[far_same * group + at].astype(F32)
                        + from_core[0, at].astype(F32)).astype(BF)
            return 0

        lax.fori_loop(0, piece, join, 0)
        over_x(h).start()
    for h in range(2):
        transform(core_dev, h)
        to_core(core_dev, 1, h).start()
    for h in range(2):
        transform(fi, h)
    for h in range(2):
        to_core(core_dev, 1, h).wait_recv()
        over_x(h).wait_recv()

        def add_up(j, _, h=h):
            at = h * piece + j
            total_ref[at] = (part[fi * group + at].astype(F32) + from_core[1, at].astype(F32)
                             + from_x[at].astype(F32))
            return 0

        lax.fori_loop(0, piece, add_up, 0)

    for k in range(CHUNKS + 1):
        send(r, k, near, near_sem.at[k]).wait_send()
        for d, p in enumerate(peers):
            send(r, k, p, send_sem.at[d, k]).wait_send()
            send(p, k, near, pass_sem.at[d, k]).wait_send()
    for h in range(2):
        to_core(far_other, 0, h).wait_send()
        to_core(core_dev, 1, h).wait_send()
        over_x(h).wait_send()


def finish(per, total_ref, bounds_ref, lag_ref, peak_ref):
    group, _, chans = total_ref.shape
    lag_id = lax.broadcasted_iota(jnp.int32, (L, chans), 0)

    def one(j, _):
        count = total_ref[j, per * L:per * L + per]
        for s in range(per):
            lag = total_ref[j, s * L:s * L + L] / count[s:s + 1]
            lag = lag.astype(BF).astype(F32)
            row = j * per + s
            inside = (lag_id >= bounds_ref[row, 0:1]) & (lag_id < bounds_ref[row, 1:2])
            peak_ref[pl.ds(row, 1), :] = jnp.max(
                jnp.where(inside, lag, -jnp.inf), axis=0, keepdims=True)
            lag_ref[row] = lag.T.astype(BF)
        return 0

    lax.fori_loop(0, group, one, 0, unroll=group <= 2)


def local(n, spectra, valid, sources, bounds):
    _, bins, rows, chans = spectra.shape
    per = sources.shape[0]
    group = n // 4
    count = bounds.shape[0]
    table = jnp.asarray(lag_table(bins, per, L))
    span = per * L + 4 * per
    vmem = pl.BlockSpec(memory_space=pltpu.VMEM)
    hbm = pl.BlockSpec(memory_space=pl.ANY)
    dma = pltpu.SemaphoreType.DMA
    half = n // 2
    total = pl.pallas_call(
        functools.partial(kernel, n),
        out_shape=jax.ShapeDtypeStruct((group, span, chans), F32),
        in_specs=[pl.BlockSpec(memory_space=pltpu.SMEM), hbm, hbm, hbm],
        out_specs=vmem,
        scratch_shapes=[
            pltpu.VMEM((2, bins, rows, chans), BF),
            pltpu.VMEM((rows, chans), jnp.int32),
            pltpu.VMEM(table.shape, BF),
            pltpu.VMEM((n, bins // 8 * 12 * per, chans), BF),
            pltpu.VMEM((n, 4 * per, 2 * chans), F32),
            pltpu.VMEM((n, 2 * bins * per, chans), BF),
            pltpu.VMEM((n, span, chans), BF),
            pltpu.VMEM((2, group, span, chans), BF),
            pltpu.VMEM((group, span, chans), BF),
            pltpu.VMEM((group, span, chans), BF),
            dma((CHUNKS,)), dma, dma,
            dma((half, CHUNKS + 1)), dma((CHUNKS + 1,)), dma((half, CHUNKS + 1)),
            dma((n, CHUNKS + 1)), dma((3, 2)), dma((3, 2)),
        ],
        compiler_params=pltpu.CompilerParams(
            collective_id=0, has_side_effects=True, vmem_limit_bytes=62 * 1024 * 1024),
    )(sources, spectra, valid, table)
    return pl.pallas_call(
        functools.partial(finish, per),
        out_shape=(jax.ShapeDtypeStruct((count, chans, L), BF),
                   jax.ShapeDtypeStruct((count, chans), F32)),
        in_specs=[vmem, vmem],
        out_specs=(vmem, vmem),
        compiler_params=pltpu.CompilerParams(vmem_limit_bytes=32 * 1024 * 1024),
    )(total, bounds.transpose(0, 2, 1))


def solution(mesh):
    in_specs = (P(None, None, "freq", "rcv"), P(None, "rcv"), P("rcv"), P("freq", "rcv", None))
    out_specs = (P("freq", "rcv", None), P("freq", "rcv"))
    return jax.shard_map(functools.partial(local, mesh.shape["rcv"]), mesh=mesh,
                         in_specs=in_specs, out_specs=out_specs, check_vma=False)
```

```python
import functools
import math

import jax
import jax.numpy as jnp
import numpy as np
from jax import lax
from jax.experimental import pallas as pl
from jax.experimental.pallas import tpu as pltpu
from jax.sharding import PartitionSpec as P

L = 128
CHUNKS = 8
EARLY = 2
MESH = pl.DeviceIdType.MESH
BF = jnp.bfloat16
F32 = jnp.float32
NT = (((1,), (1,)), ((), ()))


def lag_table(bins, per, lags):
    phase = (np.arange(1, bins + 1)[:, None] * (np.arange(lags) - lags // 2)[None, :]) % (2 * bins)
    angle = phase.astype(np.float32) * np.float32(2.0 * math.pi / (2 * bins))
    both = np.stack([np.cos(angle), -np.sin(angle)]).astype(BF).astype(np.float32)
    table = np.einsum("pft,su->stpfu", both, np.eye(per, dtype=np.float32))
    return table.reshape(per * lags, 2 * bins * per).astype(BF)


def kernel(n, sources_ref, spectra_ref, valid_ref, table_ref, total_ref,
           white, own_valid, table, onehot, picks, scales, cross, part, from_core, from_x, to_x,
           load_sem, valid_sem, table_sem, send_sem, near_sem, pass_sem, recv_sem, red_send, red_recv):
    _, bins, rows, chans = white.shape
    per = sources_ref.shape[0]
    half = n // 2
    step = bins // CHUNKS
    group = n // 4
    piece = group // 2
    fi = lax.axis_index("freq")
    r = lax.axis_index("rcv")
    x_idx, core = fi // 2, lax.rem(fi, 2)
    near = r + 1 - 2 * lax.rem(r, 2)
    peers = [lax.rem(r + 2 * d, n) for d in range(1, half)]
    core_dev = fi + 1 - 2 * core
    x_dev = lax.rem(fi + 2, 4)

    barrier = pltpu.get_barrier_semaphore()
    for dev in [(fi, near)] + [(fi, p) for p in peers] + [(core_dev, r), (x_dev, r)]:
        pl.semaphore_signal(barrier, inc=1, device_id=dev, device_id_type=MESH)

    def load(k):
        part_f = pl.ds(k * step, step)
        return pltpu.make_async_copy(spectra_ref.at[:, part_f], white.at[:, part_f], load_sem.at[k])

    for k in range(CHUNKS):
        load(k).start()
    valid_copy = pltpu.make_async_copy(valid_ref.at[pl.ds(fi * rows, rows)], own_valid, valid_sem)
    valid_copy.start()
    table_copy = pltpu.make_async_copy(table_ref, table, table_sem)
    table_copy.start()

    row_id = lax.broadcasted_iota(jnp.int32, (4 * per, chans), 0)
    lane_id = lax.broadcasted_iota(jnp.int32, (4 * per, chans), 1)
    chan_id = lax.broadcasted_iota(jnp.int32, (chans, chans), 0)
    slot_id = lax.broadcasted_iota(jnp.int32, (chans, chans), 1)
    hit = jnp.zeros((4 * per, chans), F32)
    place = jnp.zeros((chans, chans), F32)
    for s in range(per):
        off = sources_ref[s] - r * chans
        hit = jnp.where((lax.rem(row_id, per) == s) & (lane_id == off), 1.0, hit)
        place = jnp.where((lax.rem(slot_id, per) == s) & (chan_id == off), 1.0, place)
    hit = hit.astype(BF)
    for u in range(step):
        onehot[u * chans:(u + 1) * chans] = jnp.where(slot_id // per == u, place, 0.0).astype(BF)
    tile = 4 * per
    pairs = step // 8
    width = 3 * tile * pairs
    rest = chans - rows

    def send(block, k, to, sem):
        ref = scales.at[block] if k == CHUNKS else picks.at[block, pl.ds(k * width, width)]
        return pltpu.make_async_remote_copy(
            src_ref=ref, dst_ref=ref, send_sem=sem, recv_sem=recv_sem.at[block, k],
            device_id=(fi, to), device_id_type=MESH)

    def send_own(k):
        send(r, k, near, near_sem.at[k]).start()
        for d, p in enumerate(peers):
            send(r, k, p, send_sem.at[d, k]).start()

    def forward(k):
        for d, p in enumerate(peers):
            send(p, k, near, pass_sem.at[d, k]).wait_recv()
            send(p, k, near, pass_sem.at[d, k]).start()

    def arrive(k):
        send(near, k, near, near_sem.at[k]).wait_recv()
        for p in peers:
            other = p + 1 - 2 * lax.rem(p, 2)
            send(other, k, near, near_sem.at[k]).wait_recv()

    def choose(k):
        lhs = jnp.concatenate(
            [jnp.concatenate([white[0, k * step + u], white[1, k * step + u]], axis=0)
             for u in range(step)], axis=1)
        out = jnp.dot(lhs, onehot[...], preferred_element_type=F32)
        lead = out[0:chans].T
        tail = jnp.concatenate([out[chans:], out[chans:]], axis=0).T
        for i in range(pairs):
            base = k * width + i * 3 * tile
            one = slice(2 * i * tile, (2 * i + 1) * tile)
            two = slice((2 * i + 1) * tile, (2 * i + 2) * tile)
            picks[r, base:base + tile] = lead[one].astype(BF)
            picks[r, base + tile:base + 2 * tile] = lead[two].astype(BF)
            picks[r, base + 2 * tile:base + 3 * tile] = jnp.where(
                lane_id < chans // 2, tail[one], tail[two]).astype(BF)

    for k in range(EARLY):
        load(k).wait()
        choose(k)
        if k == 0:
            pl.semaphore_wait(barrier, half + 2)
        send_own(k)

    total = jnp.zeros((rows, chans), F32)
    for k in range(CHUNKS):
        if k >= EARLY:
            load(k).wait()

        def add(i, acc, k=k):
            for u in range(4):
                f = k * step + i * 4 + u
                a = white[0, f].astype(F32)
                b = white[1, f].astype(F32)
                acc = acc + (a * a + b * b)
            return acc

        total = lax.fori_loop(0, step // 4, add, total)
    valid_copy.wait()
    valid_f = own_valid[...].astype(F32)
    scale = valid_f / jnp.sqrt(total * (1.0 / bins) + 1e-6)
    valid_w = jnp.concatenate([valid_f, jnp.zeros((chans - rows, chans), F32)], axis=0).astype(BF)
    left_over = jnp.concatenate([scale, scale[0:rest], scale[rest:], scale[rest:]], axis=0)
    chosen = jnp.zeros((tile, 2 * chans), F32)
    for _ in range(3):
        high = left_over.astype(BF)
        left_over = left_over - high.astype(F32)
        chosen = chosen + lax.dot_general(hit, high, NT, preferred_element_type=F32)
    scales[r] = chosen
    send_own(CHUNKS)

    for k in range(EARLY, CHUNKS):
        choose(k)
        send_own(k)
        forward(k - EARLY)
        if k == EARLY:
            forward(CHUNKS)

    band = lax.broadcasted_iota(jnp.int32, (n, tile, chans), 1) // per
    blank = jnp.zeros((2 * chans - 2 * rows, chans), BF)

    def correlate(k):
        def one(i, _):
            base = pl.multiple_of(k * width + i * (3 * tile), tile)

            def sources_of(m, lanes):
                raw = picks[:, pl.ds(base + m * tile, tile)].astype(F32)
                return (raw * scales[:, :, lanes]).astype(BF).reshape(n * tile, chans)

            shared = sources_of(2, slice(chans, 2 * chans))
            for q in range(2):
                lhs = jnp.concatenate([sources_of(q, slice(0, chans)), shared], axis=1)
                out_re = out_im = None
                for u in range(4):
                    f = k * step + i * 8 + q * 4 + u
                    re = (white[0, f].astype(F32) * scale).astype(BF)
                    im = (white[1, f].astype(F32) * scale).astype(BF)
                    neg = -re
                    if q == 0:
                        left = jnp.concatenate([re, im, blank], axis=0)
                        right = jnp.concatenate([im, neg, blank], axis=0)
                    else:
                        left = jnp.concatenate([re, im[0:rest], blank, im[rest:]], axis=0)
                        right = jnp.concatenate([im, neg[0:rest], blank, neg[rest:]], axis=0)
                    out = jnp.dot(lhs, jnp.concatenate([left, right], axis=1),
                                  preferred_element_type=F32)
                    first = out[:, 0:chans].reshape(n, tile, chans)
                    second = out[:, chans:].reshape(n, tile, chans)
                    out_re = first if u == 0 else jnp.where(band == u, first, out_re)
                    out_im = second if u == 0 else jnp.where(band == u, second, out_im)
                at = pl.multiple_of((k * step + i * 8 + q * 4) * per, tile)
                cross[:, pl.ds(at, tile)] = out_re.astype(BF)
                cross[:, pl.ds(bins * per + at, tile)] = out_im.astype(BF)
            return 0

        lax.fori_loop(0, pairs, one, 0)

    body = per * L
    for k in range(CHUNKS):
        if k + CHUNKS - EARLY < CHUNKS:
            forward(k + CHUNKS - EARLY)
        if k == 0:
            arrive(CHUNKS)
            usable = jnp.where(scales[:, :, 0:chans] > 0.0, 1.0, 0.0)
            counts = jnp.dot(usable.astype(BF).reshape(n * tile, chans), valid_w,
                             preferred_element_type=F32)
            part[:, body:body + tile] = counts.reshape(n, tile, chans).astype(BF)
        arrive(k)
        correlate(k)
    table_copy.wait()

    def transform(i):
        def one(j, _):
            at = i * group + 2 * j
            both = jnp.dot(table[...], jnp.concatenate([cross[at], cross[at + 1]], axis=1),
                           preferred_element_type=F32)
            part[at, 0:body] = both[:, 0:chans].astype(BF)
            part[at + 1, 0:body] = both[:, chans:].astype(BF)
            return 0

        lax.fori_loop(0, piece, one, 0)

    def to_core(i, slot, h):
        return pltpu.make_async_remote_copy(
            src_ref=part.at[pl.ds(i * group + h * piece, piece)],
            dst_ref=from_core.at[slot, pl.ds(h * piece, piece)],
            send_sem=red_send.at[slot, h], recv_sem=red_recv.at[slot, h],
            device_id=(core_dev, r), device_id_type=MESH)

    def over_x(h):
        mine = pl.ds(h * piece, piece)
        return pltpu.make_async_remote_copy(
            src_ref=to_x.at[mine], dst_ref=from_x.at[mine],
            send_sem=red_send.at[2, h], recv_sem=red_recv.at[2, h],
            device_id=(x_dev, r), device_id_type=MESH)

    far_other = 2 * (1 - x_idx) + (1 - core)
    far_same = 2 * (1 - x_idx) + core
    transform(far_other)
    for h in range(2):
        to_core(far_other, 0, h).start()
    transform(far_same)
    for h in range(2):
        to_core(far_other, 0, h).wait_recv()

        def join(j, _, h=h):
            at = h * piece + j
            to_x[at] = (part[far_same * group + at].astype(F32)
                        + from_core[0, at].astype(F32)).astype(BF)
            return 0

        lax.fori_loop(0, piece, join, 0)
        over_x(h).start()
    transform(core_dev)
    for h in range(2):
        to_core(core_dev, 1, h).start()
    transform(fi)
    for h in range(2):
        to_core(core_dev, 1, h).wait_recv()
        over_x(h).wait_recv()

        def add_up(j, _, h=h):
            at = h * piece + j
            total_ref[at] = (part[fi * group + at].astype(F32) + from_core[1, at].astype(F32)
                             + from_x[at].astype(F32))
            return 0

        lax.fori_loop(0, piece, add_up, 0)

    for k in range(CHUNKS + 1):
        send(r, k, near, near_sem.at[k]).wait_send()
        for d, p in enumerate(peers):
            send(r, k, p, send_sem.at[d, k]).wait_send()
            send(p, k, near, pass_sem.at[d, k]).wait_send()
    for h in range(2):
        to_core(far_other, 0, h).wait_send()
        to_core(core_dev, 1, h).wait_send()
        over_x(h).wait_send()


def finish(per, total_ref, bounds_ref, lag_ref, peak_ref):
    group, _, chans = total_ref.shape
    lag_id = lax.broadcasted_iota(jnp.int32, (L, chans), 0)

    def one(j, _):
        count = total_ref[j, per * L:per * L + per]
        for s in range(per):
            lag = total_ref[j, s * L:s * L + L] / count[s:s + 1]
            lag = lag.astype(BF).astype(F32)
            row = j * per + s
            inside = (lag_id >= bounds_ref[row, 0:1]) & (lag_id < bounds_ref[row, 1:2])
            peak_ref[pl.ds(row, 1), :] = jnp.max(
                jnp.where(inside, lag, -jnp.inf), axis=0, keepdims=True)
            lag_ref[row] = lag.T.astype(BF)
        return 0

    lax.fori_loop(0, group, one, 0, unroll=group <= 2)


def local(n, spectra, valid, sources, bounds):
    _, bins, rows, chans = spectra.shape
    per = sources.shape[0]
    group = n // 4
    count = bounds.shape[0]
    table = jnp.asarray(lag_table(bins, per, L))
    span = per * L + 4 * per
    vmem = pl.BlockSpec(memory_space=pltpu.VMEM)
    hbm = pl.BlockSpec(memory_space=pl.ANY)
    dma = pltpu.SemaphoreType.DMA
    half = n // 2
    total = pl.pallas_call(
        functools.partial(kernel, n),
        out_shape=jax.ShapeDtypeStruct((group, span, chans), F32),
        in_specs=[pl.BlockSpec(memory_space=pltpu.SMEM), hbm, hbm, hbm],
        out_specs=vmem,
        scratch_shapes=[
            pltpu.VMEM((2, bins, rows, chans), BF),
            pltpu.VMEM((rows, chans), jnp.int32),
            pltpu.VMEM(table.shape, BF),
            pltpu.VMEM((bins // CHUNKS * chans, chans), BF),
            pltpu.VMEM((n, bins // 8 * 12 * per, chans), BF),
            pltpu.VMEM((n, 4 * per, 2 * chans), F32),
            pltpu.VMEM((n, 2 * bins * per, chans), BF),
            pltpu.VMEM((n, span, chans), BF),
            pltpu.VMEM((2, group, span, chans), BF),
            pltpu.VMEM((group, span, chans), BF),
            pltpu.VMEM((group, span, chans), BF),
            dma((CHUNKS,)), dma, dma,
            dma((half, CHUNKS + 1)), dma((CHUNKS + 1,)), dma((half, CHUNKS + 1)),
            dma((n, CHUNKS + 1)), dma((3, 2)), dma((3, 2)),
        ],
        compiler_params=pltpu.CompilerParams(
            collective_id=0, has_side_effects=True, vmem_limit_bytes=62 * 1024 * 1024),
    )(sources, spectra, valid, table)
    return pl.pallas_call(
        functools.partial(finish, per),
        out_shape=(jax.ShapeDtypeStruct((count, chans, L), BF),
                   jax.ShapeDtypeStruct((count, chans), F32)),
        in_specs=[vmem, vmem],
        out_specs=(vmem, vmem),
        compiler_params=pltpu.CompilerParams(vmem_limit_bytes=32 * 1024 * 1024),
    )(total, bounds.transpose(0, 2, 1))


def solution(mesh):
    in_specs = (P(None, None, "freq", "rcv"), P(None, "rcv"), P("rcv"), P("freq", "rcv", None))
    out_specs = (P("freq", "rcv", None), P("freq", "rcv"))
    return jax.shard_map(functools.partial(local, mesh.shape["rcv"]), mesh=mesh,
                         in_specs=in_specs, out_specs=out_specs, check_vma=False)
```

```python
import functools
import math

import jax
import jax.numpy as jnp
import numpy as np
from jax import lax
from jax.experimental import pallas as pl
from jax.experimental.pallas import tpu as pltpu
from jax.sharding import PartitionSpec as P

L = 128
CHUNKS = 8
EARLY = 3
AHEAD = 3
MESH = pl.DeviceIdType.MESH
BF = jnp.bfloat16
F32 = jnp.float32
NT = (((1,), (1,)), ((), ()))


def lag_table(bins, per, lags):
    phase = (np.arange(1, bins + 1)[:, None] * (np.arange(lags) - lags // 2)[None, :]) % (2 * bins)
    angle = phase.astype(np.float32) * np.float32(2.0 * math.pi / (2 * bins))
    both = np.stack([np.cos(angle), -np.sin(angle)]).astype(BF).astype(np.float32)
    table = np.einsum("pft,su->stpfu", both, np.eye(per, dtype=np.float32))
    return table.reshape(per * lags, 2 * bins * per).astype(BF)


def kernel(n, sources_ref, spectra_ref, valid_ref, table_ref, total_ref,
           white, own_valid, table, onehot, picks, scales, spread, cross, part, from_core, from_x, to_x,
           load_sem, valid_sem, table_sem, send_sem, near_sem, pass_sem, recv_sem, red_send, red_recv):
    _, bins, rows, chans = white.shape
    per = sources_ref.shape[0]
    half = n // 2
    step = bins // CHUNKS
    group = n // 4
    piece = group // 2
    fi = lax.axis_index("freq")
    r = lax.axis_index("rcv")
    x_idx, core = fi // 2, lax.rem(fi, 2)
    near = r + 1 - 2 * lax.rem(r, 2)
    first_block = r // group
    blocks = [lax.rem(first_block + o, 4) for o in range(4)]

    def column(o):
        inner = lax.rem(r, group) // 2
        return [blocks[o] * group + 2 * lax.rem(inner + t, piece) + lax.rem(r, 2)
                for t in range(piece) if (o, t) != (0, 0)]

    halves = [column(0) + column(2), column(1) + column(3)]
    peers = halves[0] + halves[1]
    ranges = [range(len(halves[0])), range(len(halves[0]), len(peers))]
    core_dev = fi + 1 - 2 * core
    x_dev = lax.rem(fi + 2, 4)

    barrier = pltpu.get_barrier_semaphore()
    for dev in [(fi, near)] + [(fi, p) for p in peers] + [(core_dev, r), (x_dev, r)]:
        pl.semaphore_signal(barrier, inc=1, device_id=dev, device_id_type=MESH)

    def load(k):
        part_f = pl.ds(k * step, step)
        return pltpu.make_async_copy(spectra_ref.at[:, part_f], white.at[:, part_f], load_sem.at[k])

    for k in range(CHUNKS):
        load(k).start()
    valid_copy = pltpu.make_async_copy(valid_ref.at[pl.ds(fi * rows, rows)], own_valid, valid_sem)
    valid_copy.start()
    table_copy = pltpu.make_async_copy(table_ref, table, table_sem)
    table_copy.start()

    row_id = lax.broadcasted_iota(jnp.int32, (4 * per, chans), 0)
    lane_id = lax.broadcasted_iota(jnp.int32, (4 * per, chans), 1)
    chan_id = lax.broadcasted_iota(jnp.int32, (chans, chans), 0)
    slot_id = lax.broadcasted_iota(jnp.int32, (chans, chans), 1)
    hit = jnp.zeros((4 * per, chans), F32)
    place = jnp.zeros((chans, chans), F32)
    for s in range(per):
        off = sources_ref[s] - r * chans
        hit = jnp.where((lax.rem(row_id, per) == s) & (lane_id == off), 1.0, hit)
        place = jnp.where((lax.rem(slot_id, per) == s) & (chan_id == off), 1.0, place)
    hit = hit.astype(BF)
    for u in range(step):
        onehot[u * chans:(u + 1) * chans] = jnp.where(slot_id // per == u, place, 0.0).astype(BF)
    tile = 4 * per
    pairs = step // 8
    width = 3 * tile * pairs
    rest = chans - rows

    def send(block, k, to, sem):
        ref = scales.at[block] if k == CHUNKS else picks.at[block, pl.ds(k * width, width)]
        return pltpu.make_async_remote_copy(
            src_ref=ref, dst_ref=ref, send_sem=sem, recv_sem=recv_sem.at[block, k],
            device_id=(fi, to), device_id_type=MESH)

    def send_own(k, g):
        if g == 0:
            send(r, k, near, near_sem.at[k]).start()
        for d in ranges[g]:
            send(r, k, peers[d], send_sem.at[d, k]).start()

    def forward(k, g):
        for d in ranges[g]:
            send(peers[d], k, near, pass_sem.at[d, k]).wait_recv()
            send(peers[d], k, near, pass_sem.at[d, k]).start()

    def arrive(k, g):
        if g == 0:
            send(near, k, near, near_sem.at[k]).wait_recv()
        for p in halves[g]:
            other = p + 1 - 2 * lax.rem(p, 2)
            send(other, k, near, near_sem.at[k]).wait_recv()

    def choose(k):
        lhs = jnp.concatenate(
            [jnp.concatenate([white[0, k * step + u], white[1, k * step + u]], axis=0)
             for u in range(step)], axis=1)
        out = jnp.dot(lhs, onehot[...], preferred_element_type=F32)
        lead = out[0:chans].T
        tail = jnp.concatenate([out[chans:], out[chans:]], axis=0).T
        for i in range(pairs):
            base = k * width + i * 3 * tile
            one = slice(2 * i * tile, (2 * i + 1) * tile)
            two = slice((2 * i + 1) * tile, (2 * i + 2) * tile)
            picks[r, base:base + tile] = lead[one].astype(BF)
            picks[r, base + tile:base + 2 * tile] = lead[two].astype(BF)
            picks[r, base + 2 * tile:base + 3 * tile] = jnp.where(
                lane_id < chans // 2, tail[one], tail[two]).astype(BF)

    for k in range(EARLY):
        load(k).wait()
        choose(k)
        if k == 0:
            pl.semaphore_wait(barrier, half + 2)
        send_own(k, 0)

    total = jnp.zeros((rows, chans), F32)
    for k in range(CHUNKS):
        if k >= EARLY:
            load(k).wait()

        def add(i, acc, k=k):
            for u in range(4):
                f = k * step + i * 4 + u
                a = white[0, f].astype(F32)
                b = white[1, f].astype(F32)
                acc = acc + (a * a + b * b)
            return acc

        total = lax.fori_loop(0, step // 4, add, total)
    valid_copy.wait()
    valid_f = own_valid[...].astype(F32)
    scale = valid_f / jnp.sqrt(total * (1.0 / bins) + 1e-6)
    valid_w = jnp.concatenate([valid_f, jnp.zeros((chans - rows, chans), F32)], axis=0).astype(BF)
    left_over = jnp.concatenate([scale, scale[0:rest]], axis=0)
    chosen = jnp.zeros((tile, chans), F32)
    for _ in range(3):
        high = left_over.astype(BF)
        left_over = left_over - high.astype(F32)
        chosen = chosen + lax.dot_general(hit, high, NT, preferred_element_type=F32)
    scales[r] = chosen[0:2 * per]
    send_own(CHUNKS, 0)
    send_own(CHUNKS, 1)

    for k in range(EARLY, CHUNKS):
        choose(k)
        send_own(k, 0)
    for k in range(CHUNKS):
        send_own(k, 1)
    order = [(k, g) for g in range(2) for k in range(CHUNKS)]
    for k, g in order[:AHEAD]:
        forward(k, g)
    forward(CHUNKS, 0)
    forward(CHUNKS, 1)

    band = lax.broadcasted_iota(jnp.int32, (half, tile, chans), 1) // per
    blank = jnp.zeros((2 * chans - 2 * rows, chans), BF)

    def correlate(k, g):
        owned = [pl.ds(blocks[g + o] * group, group) for o in (0, 2)]

        def one(i, _):
            base = pl.multiple_of(k * width + i * (3 * tile), tile)

            def sources_of(at, m):
                return jnp.concatenate([
                    (picks[o, pl.ds(base + at * tile, tile)].astype(F32) * spread[m, o]).astype(BF)
                    for o in owned], axis=0).reshape(half * tile, chans)

            shared = sources_of(2, 1)
            for q in range(2):
                lhs = jnp.concatenate([sources_of(q, 0), shared], axis=1)
                out_re = out_im = None
                for u in range(4):
                    f = k * step + i * 8 + q * 4 + u
                    re = (white[0, f].astype(F32) * scale).astype(BF)
                    im = (white[1, f].astype(F32) * scale).astype(BF)
                    neg = -re
                    if q == 0:
                        left = jnp.concatenate([re, im, blank], axis=0)
                        right = jnp.concatenate([im, neg, blank], axis=0)
                    else:
                        left = jnp.concatenate([re, im[0:rest], blank, im[rest:]], axis=0)
                        right = jnp.concatenate([im, neg[0:rest], blank, neg[rest:]], axis=0)
                    out = jnp.dot(lhs, jnp.concatenate([left, right], axis=1),
                                  preferred_element_type=F32)
                    first = out[:, 0:chans].reshape(half, tile, chans)
                    second = out[:, chans:].reshape(half, tile, chans)
                    out_re = first if u == 0 else jnp.where(band == u, first, out_re)
                    out_im = second if u == 0 else jnp.where(band == u, second, out_im)
                at = pl.multiple_of((k * step + i * 8 + q * 4) * per, tile)
                for m, o in enumerate(owned):
                    mine = slice(m * group, (m + 1) * group)
                    cross[o, pl.ds(at, tile)] = out_re[mine].astype(BF)
                    cross[o, pl.ds(bins * per + at, tile)] = out_im[mine].astype(BF)
            return 0

        lax.fori_loop(0, pairs, one, 0)

    body = per * L
    arrive(CHUNKS, 0)
    arrive(CHUNKS, 1)
    every = scales[...].reshape(n * 2 * per, chans)
    lane = lax.broadcasted_iota(jnp.int32, every.shape, 1)
    low = jnp.where(lane < chans // 2, pltpu.roll(every, rows, 1), pltpu.roll(every, rest, 1))
    for m, src in enumerate((every, low)):
        src = src.reshape(n, 2 * per, chans)
        spread[m] = jnp.concatenate([src, src], axis=1)
    usable = jnp.where(spread[0] > 0.0, 1.0, 0.0)
    counts = jnp.dot(usable.astype(BF).reshape(n * tile, chans), valid_w,
                     preferred_element_type=F32)
    part[:, body:body + tile] = counts.reshape(n, tile, chans).astype(BF)

    def transform(i):
        def one(j, _):
            at = i * group + 2 * j
            both = jnp.dot(table[...], jnp.concatenate([cross[at], cross[at + 1]], axis=1),
                           preferred_element_type=F32)
            part[at, 0:body] = both[:, 0:chans].astype(BF)
            part[at + 1, 0:body] = both[:, chans:].astype(BF)
            return 0

        lax.fori_loop(0, piece, one, 0)

    def to_core(i, slot, h):
        return pltpu.make_async_remote_copy(
            src_ref=part.at[pl.ds(i * group + h * piece, piece)],
            dst_ref=from_core.at[slot, pl.ds(h * piece, piece)],
            send_sem=red_send.at[slot, h], recv_sem=red_recv.at[slot, h],
            device_id=(core_dev, r), device_id_type=MESH)

    def over_x(h):
        mine = pl.ds(h * piece, piece)
        return pltpu.make_async_remote_copy(
            src_ref=to_x.at[mine], dst_ref=from_x.at[mine],
            send_sem=red_send.at[2, h], recv_sem=red_recv.at[2, h],
            device_id=(x_dev, r), device_id_type=MESH)

    far_other = 2 * (1 - x_idx) + (1 - core)
    far_same = 2 * (1 - x_idx) + core

    def gather_sums():
        transform(far_same)
        for h in range(2):
            to_core(far_other, 0, h).wait_recv()

            def join(j, _, h=h):
                at = h * piece + j
                to_x[at] = (part[far_same * group + at].astype(F32)
                            + from_core[0, at].astype(F32)).astype(BF)
                return 0

            lax.fori_loop(0, piece, join, 0)
            over_x(h).start()
        transform(fi)

    def give_sums():
        transform(far_other)
        for h in range(2):
            to_core(far_other, 0, h).start()
        transform(core_dev)
        for h in range(2):
            to_core(core_dev, 1, h).start()

    for m, (k, g) in enumerate(order):
        if m + AHEAD < len(order):
            forward(*order[m + AHEAD])
        arrive(k, g)
        correlate(k, g)
        if k == CHUNKS - 1:
            if g == 0:
                table_copy.wait()
            mine = core == lax.rem(first_block + g, 2)
            pl.when(mine)(gather_sums)
            pl.when(jnp.logical_not(mine))(give_sums)
    for h in range(2):
        to_core(core_dev, 1, h).wait_recv()
        over_x(h).wait_recv()

        def add_up(j, _, h=h):
            at = h * piece + j
            total_ref[at] = (part[fi * group + at].astype(F32) + from_core[1, at].astype(F32)
                             + from_x[at].astype(F32))
            return 0

        lax.fori_loop(0, piece, add_up, 0)

    for k in range(CHUNKS + 1):
        send(r, k, near, near_sem.at[k]).wait_send()
        for d, p in enumerate(peers):
            send(r, k, p, send_sem.at[d, k]).wait_send()
            send(p, k, near, pass_sem.at[d, k]).wait_send()
    for h in range(2):
        to_core(far_other, 0, h).wait_send()
        to_core(core_dev, 1, h).wait_send()
        over_x(h).wait_send()


def finish(per, total_ref, bounds_ref, lag_ref, peak_ref):
    group, _, chans = total_ref.shape
    lag_id = lax.broadcasted_iota(jnp.int32, (L, chans), 0)

    def one(j, _):
        count = total_ref[j, per * L:per * L + per]
        for s in range(per):
            lag = total_ref[j, s * L:s * L + L] / count[s:s + 1]
            lag = lag.astype(BF).astype(F32)
            row = j * per + s
            inside = (lag_id >= bounds_ref[row, 0:1]) & (lag_id < bounds_ref[row, 1:2])
            peak_ref[pl.ds(row, 1), :] = jnp.max(
                jnp.where(inside, lag, -jnp.inf), axis=0, keepdims=True)
            lag_ref[row] = lag.T.astype(BF)
        return 0

    lax.fori_loop(0, group, one, 0, unroll=group <= 2)


def local(n, spectra, valid, sources, bounds):
    _, bins, rows, chans = spectra.shape
    per = sources.shape[0]
    group = n // 4
    count = bounds.shape[0]
    table = jnp.asarray(lag_table(bins, per, L))
    span = per * L + 4 * per
    vmem = pl.BlockSpec(memory_space=pltpu.VMEM)
    hbm = pl.BlockSpec(memory_space=pl.ANY)
    dma = pltpu.SemaphoreType.DMA
    half = n // 2
    total = pl.pallas_call(
        functools.partial(kernel, n),
        out_shape=jax.ShapeDtypeStruct((group, span, chans), F32),
        in_specs=[pl.BlockSpec(memory_space=pltpu.SMEM), hbm, hbm, hbm],
        out_specs=vmem,
        scratch_shapes=[
            pltpu.VMEM((2, bins, rows, chans), BF),
            pltpu.VMEM((rows, chans), jnp.int32),
            pltpu.VMEM(table.shape, BF),
            pltpu.VMEM((bins // CHUNKS * chans, chans), BF),
            pltpu.VMEM((n, bins // 8 * 12 * per, chans), BF),
            pltpu.VMEM((n, 2 * per, chans), F32),
            pltpu.VMEM((2, n, 4 * per, chans), F32),
            pltpu.VMEM((n, 2 * bins * per, chans), BF),
            pltpu.VMEM((n, span, chans), BF),
            pltpu.VMEM((2, group, span, chans), BF),
            pltpu.VMEM((group, span, chans), BF),
            pltpu.VMEM((group, span, chans), BF),
            dma((CHUNKS,)), dma, dma,
            dma((half, CHUNKS + 1)), dma((CHUNKS + 1,)), dma((half, CHUNKS + 1)),
            dma((n, CHUNKS + 1)), dma((3, 2)), dma((3, 2)),
        ],
        compiler_params=pltpu.CompilerParams(
            collective_id=0, has_side_effects=True, vmem_limit_bytes=62 * 1024 * 1024),
    )(sources, spectra, valid, table)
    return pl.pallas_call(
        functools.partial(finish, per),
        out_shape=(jax.ShapeDtypeStruct((count, chans, L), BF),
                   jax.ShapeDtypeStruct((count, chans), F32)),
        in_specs=[vmem, vmem],
        out_specs=(vmem, vmem),
        compiler_params=pltpu.CompilerParams(vmem_limit_bytes=32 * 1024 * 1024),
    )(total, bounds.transpose(0, 2, 1))


def solution(mesh):
    in_specs = (P(None, None, "freq", "rcv"), P(None, "rcv"), P("rcv"), P("freq", "rcv", None))
    out_specs = (P("freq", "rcv", None), P("freq", "rcv"))
    return jax.shard_map(functools.partial(local, mesh.shape["rcv"]), mesh=mesh,
                         in_specs=in_specs, out_specs=out_specs, check_vma=False)
```

```python
import functools
import math

import jax
import jax.numpy as jnp
import numpy as np
from jax import lax
from jax.experimental import pallas as pl
from jax.experimental.pallas import tpu as pltpu
from jax.sharding import PartitionSpec as P

L = 128
CHUNKS = 8
EARLY = 3
AHEAD = 5
MESH = pl.DeviceIdType.MESH
BF = jnp.bfloat16
F32 = jnp.float32
NT = (((1,), (1,)), ((), ()))


def lag_table(bins, per, lags):
    phase = (np.arange(1, bins + 1)[:, None] * (np.arange(lags) - lags // 2)[None, :]) % (2 * bins)
    angle = phase.astype(np.float32) * np.float32(2.0 * math.pi / (2 * bins))
    both = np.stack([np.cos(angle), -np.sin(angle)]).astype(BF).astype(np.float32)
    table = np.einsum("pft,su->stpfu", both, np.eye(per, dtype=np.float32))
    return table.reshape(per * lags, 2 * bins * per).astype(BF)


def kernel(n, sources_ref, spectra_ref, valid_ref, table_ref, total_ref,
           white, own_valid, table, onehot, picks, scales, spread, cross, part, from_core, from_x, to_x,
           load_sem, valid_sem, table_sem, send_sem, near_sem, pass_sem, recv_sem, red_send, red_recv):
    _, bins, rows, chans = white.shape
    per = sources_ref.shape[0]
    half = n // 2
    step = bins // CHUNKS
    group = n // 4
    piece = group // 2
    fi = lax.axis_index("freq")
    r = lax.axis_index("rcv")
    x_idx, core = fi // 2, lax.rem(fi, 2)
    near = r + 1 - 2 * lax.rem(r, 2)
    first_block = r // group
    blocks = [lax.rem(first_block + o, 4) for o in range(4)]

    def column(o):
        inner = lax.rem(r, group) // 2
        return [blocks[o] * group + 2 * lax.rem(inner + t, piece) + lax.rem(r, 2)
                for t in range(piece) if (o, t) != (0, 0)]

    halves = [column(0) + column(2), column(1) + column(3)]
    peers = halves[0] + halves[1]
    ranges = [range(len(halves[0])), range(len(halves[0]), len(peers))]
    core_dev = fi + 1 - 2 * core
    x_dev = lax.rem(fi + 2, 4)

    barrier = pltpu.get_barrier_semaphore()
    for dev in [(fi, near)] + [(fi, p) for p in peers] + [(core_dev, r), (x_dev, r)]:
        pl.semaphore_signal(barrier, inc=1, device_id=dev, device_id_type=MESH)

    def load(k):
        part_f = pl.ds(k * step, step)
        return pltpu.make_async_copy(spectra_ref.at[:, part_f], white.at[:, part_f], load_sem.at[k])

    for k in range(CHUNKS):
        load(k).start()
    valid_copy = pltpu.make_async_copy(valid_ref.at[pl.ds(fi * rows, rows)], own_valid, valid_sem)
    valid_copy.start()
    table_copy = pltpu.make_async_copy(table_ref, table, table_sem)
    table_copy.start()

    row_id = lax.broadcasted_iota(jnp.int32, (4 * per, chans), 0)
    lane_id = lax.broadcasted_iota(jnp.int32, (4 * per, chans), 1)
    chan_id = lax.broadcasted_iota(jnp.int32, (chans, chans), 0)
    slot_id = lax.broadcasted_iota(jnp.int32, (chans, chans), 1)
    hit = jnp.zeros((4 * per, chans), F32)
    place = jnp.zeros((chans, chans), F32)
    for s in range(per):
        off = sources_ref[s] - r * chans
        hit = jnp.where((lax.rem(row_id, per) == s) & (lane_id == off), 1.0, hit)
        place = jnp.where((lax.rem(slot_id, per) == s) & (chan_id == off), 1.0, place)
    hit = hit.astype(BF)
    for u in range(step):
        onehot[u * chans:(u + 1) * chans] = jnp.where(slot_id // per == u, place, 0.0).astype(BF)
    tile = 4 * per
    pairs = step // 8
    width = 3 * tile * pairs
    rest = chans - rows

    def send(block, k, to, sem):
        ref = scales.at[block] if k == CHUNKS else picks.at[block, pl.ds(k * width, width)]
        return pltpu.make_async_remote_copy(
            src_ref=ref, dst_ref=ref, send_sem=sem, recv_sem=recv_sem.at[block, k],
            device_id=(fi, to), device_id_type=MESH)

    def send_own(k, g):
        if g == 0:
            send(r, k, near, near_sem.at[k]).start()
        for d in ranges[g]:
            send(r, k, peers[d], send_sem.at[d, k]).start()

    def forward(k, g):
        for d in ranges[g]:
            send(peers[d], k, near, pass_sem.at[d, k]).wait_recv()
            send(peers[d], k, near, pass_sem.at[d, k]).start()

    def arrive(k, g):
        if g == 0:
            send(near, k, near, near_sem.at[k]).wait_recv()
        for p in halves[g]:
            other = p + 1 - 2 * lax.rem(p, 2)
            send(other, k, near, near_sem.at[k]).wait_recv()

    def choose(k):
        lhs = jnp.concatenate(
            [jnp.concatenate([white[0, k * step + u], white[1, k * step + u]], axis=0)
             for u in range(step)], axis=1)
        out = jnp.dot(lhs, onehot[...], preferred_element_type=F32)
        lead = out[0:chans].T
        tail = jnp.concatenate([out[chans:], out[chans:]], axis=0).T
        for i in range(pairs):
            base = k * width + i * 3 * tile
            one = slice(2 * i * tile, (2 * i + 1) * tile)
            two = slice((2 * i + 1) * tile, (2 * i + 2) * tile)
            picks[r, base:base + tile] = lead[one].astype(BF)
            picks[r, base + tile:base + 2 * tile] = lead[two].astype(BF)
            picks[r, base + 2 * tile:base + 3 * tile] = jnp.where(
                lane_id < chans // 2, tail[one], tail[two]).astype(BF)

    for k in range(EARLY):
        load(k).wait()
        choose(k)
        if k == 0:
            pl.semaphore_wait(barrier, half + 2)
        send_own(k, 0)

    total = jnp.zeros((rows, chans), F32)
    for k in range(CHUNKS):
        if k >= EARLY:
            load(k).wait()

        def add(i, acc, k=k):
            for u in range(4):
                f = k * step + i * 4 + u
                a = white[0, f].astype(F32)
                b = white[1, f].astype(F32)
                acc = acc + (a * a + b * b)
            return acc

        total = lax.fori_loop(0, step // 4, add, total)
    valid_copy.wait()
    valid_f = own_valid[...].astype(F32)
    scale = valid_f / jnp.sqrt(total * (1.0 / bins) + 1e-6)
    valid_w = jnp.concatenate([valid_f, jnp.zeros((chans - rows, chans), F32)], axis=0).astype(BF)
    left_over = jnp.concatenate([scale, scale[0:rest]], axis=0)
    chosen = jnp.zeros((tile, chans), F32)
    for _ in range(3):
        high = left_over.astype(BF)
        left_over = left_over - high.astype(F32)
        chosen = chosen + lax.dot_general(hit, high, NT, preferred_element_type=F32)
    scales[r] = chosen[0:2 * per]
    send_own(CHUNKS, 0)
    send_own(CHUNKS, 1)

    for k in range(EARLY, CHUNKS):
        choose(k)
        send_own(k, 0)
    for k in range(CHUNKS):
        send_own(k, 1)
    order = [(k, g) for g in range(2) for k in range(CHUNKS)]
    for k, g in order[:AHEAD]:
        forward(k, g)
    forward(CHUNKS, 0)
    forward(CHUNKS, 1)

    band = lax.broadcasted_iota(jnp.int32, (half, tile, chans), 1) // per
    blank = jnp.zeros((2 * chans - 2 * rows, chans), BF)

    def correlate(k, g):
        owned = [pl.ds(blocks[g + o] * group, group) for o in (0, 2)]

        def one(i, _):
            base = pl.multiple_of(k * width + i * (3 * tile), tile)

            def sources_of(at, m):
                return jnp.concatenate([
                    (picks[o, pl.ds(base + at * tile, tile)].astype(F32) * spread[m, o]).astype(BF)
                    for o in owned], axis=0).reshape(half * tile, chans)

            shared = sources_of(2, 1)
            for q in range(2):
                lhs = jnp.concatenate([sources_of(q, 0), shared], axis=1)
                out_re = out_im = None
                for u in range(4):
                    f = k * step + i * 8 + q * 4 + u
                    re = (white[0, f].astype(F32) * scale).astype(BF)
                    im = (white[1, f].astype(F32) * scale).astype(BF)
                    neg = -re
                    if q == 0:
                        left = jnp.concatenate([re, im, blank], axis=0)
                        right = jnp.concatenate([im, neg, blank], axis=0)
                    else:
                        left = jnp.concatenate([re, im[0:rest], blank, im[rest:]], axis=0)
                        right = jnp.concatenate([im, neg[0:rest], blank, neg[rest:]], axis=0)
                    out = jnp.dot(lhs, jnp.concatenate([left, right], axis=1),
                                  preferred_element_type=F32)
                    first = out[:, 0:chans].reshape(half, tile, chans)
                    second = out[:, chans:].reshape(half, tile, chans)
                    out_re = first if u == 0 else jnp.where(band == u, first, out_re)
                    out_im = second if u == 0 else jnp.where(band == u, second, out_im)
                at = pl.multiple_of((k * step + i * 8 + q * 4) * per, tile)
                for m, o in enumerate(owned):
                    mine = slice(m * group, (m + 1) * group)
                    cross[o, pl.ds(at, tile)] = out_re[mine].astype(BF)
                    cross[o, pl.ds(bins * per + at, tile)] = out_im[mine].astype(BF)
            return 0

        lax.fori_loop(0, pairs, one, 0)

    body = per * L
    arrive(CHUNKS, 0)
    arrive(CHUNKS, 1)
    every = scales[...].reshape(n * 2 * per, chans)
    lane = lax.broadcasted_iota(jnp.int32, every.shape, 1)
    low = jnp.where(lane < chans // 2, pltpu.roll(every, rows, 1), pltpu.roll(every, rest, 1))
    for m, src in enumerate((every, low)):
        src = src.reshape(n, 2 * per, chans)
        spread[m] = jnp.concatenate([src, src], axis=1)
    usable = jnp.where(spread[0] > 0.0, 1.0, 0.0)
    counts = jnp.dot(usable.astype(BF).reshape(n * tile, chans), valid_w,
                     preferred_element_type=F32)
    part[:, body:body + tile] = counts.reshape(n, tile, chans).astype(BF)

    def transform(i):
        def one(j, _):
            at = i * group + 2 * j
            both = jnp.dot(table[...], jnp.concatenate([cross[at], cross[at + 1]], axis=1),
                           preferred_element_type=F32)
            part[at, 0:body] = both[:, 0:chans].astype(BF)
            part[at + 1, 0:body] = both[:, chans:].astype(BF)
            return 0

        lax.fori_loop(0, piece, one, 0)

    def to_core(i, slot, h):
        return pltpu.make_async_remote_copy(
            src_ref=part.at[pl.ds(i * group + h * piece, piece)],
            dst_ref=from_core.at[slot, pl.ds(h * piece, piece)],
            send_sem=red_send.at[slot, h], recv_sem=red_recv.at[slot, h],
            device_id=(core_dev, r), device_id_type=MESH)

    def over_x(h):
        mine = pl.ds(h * piece, piece)
        return pltpu.make_async_remote_copy(
            src_ref=to_x.at[mine], dst_ref=from_x.at[mine],
            send_sem=red_send.at[2, h], recv_sem=red_recv.at[2, h],
            device_id=(x_dev, r), device_id_type=MESH)

    far_other = 2 * (1 - x_idx) + (1 - core)
    far_same = 2 * (1 - x_idx) + core

    def gather_sums():
        transform(far_same)
        for h in range(2):
            to_core(far_other, 0, h).wait_recv()

            def join(j, _, h=h):
                at = h * piece + j
                to_x[at] = (part[far_same * group + at].astype(F32)
                            + from_core[0, at].astype(F32)).astype(BF)
                return 0

            lax.fori_loop(0, piece, join, 0)
            over_x(h).start()
        transform(fi)

    def give_sums():
        transform(far_other)
        for h in range(2):
            to_core(far_other, 0, h).start()
        transform(core_dev)
        for h in range(2):
            to_core(core_dev, 1, h).start()

    for m, (k, g) in enumerate(order):
        if m + AHEAD < len(order):
            forward(*order[m + AHEAD])
        arrive(k, g)
        correlate(k, g)
        if k == CHUNKS - 1:
            if g == 0:
                table_copy.wait()
            mine = core == lax.rem(first_block + g, 2)
            pl.when(mine)(gather_sums)
            pl.when(jnp.logical_not(mine))(give_sums)
    for h in range(2):
        to_core(core_dev, 1, h).wait_recv()
        over_x(h).wait_recv()

        def add_up(j, _, h=h):
            at = h * piece + j
            total_ref[at] = (part[fi * group + at].astype(F32) + from_core[1, at].astype(F32)
                             + from_x[at].astype(F32))
            return 0

        lax.fori_loop(0, piece, add_up, 0)

    for k in range(CHUNKS + 1):
        send(r, k, near, near_sem.at[k]).wait_send()
        for d, p in enumerate(peers):
            send(r, k, p, send_sem.at[d, k]).wait_send()
            send(p, k, near, pass_sem.at[d, k]).wait_send()
    for h in range(2):
        to_core(far_other, 0, h).wait_send()
        to_core(core_dev, 1, h).wait_send()
        over_x(h).wait_send()


def finish(per, total_ref, bounds_ref, lag_ref, peak_ref):
    group, _, chans = total_ref.shape
    lag_id = lax.broadcasted_iota(jnp.int32, (L, chans), 0)

    def one(j, _):
        count = total_ref[j, per * L:per * L + per]
        for s in range(per):
            lag = total_ref[j, s * L:s * L + L] / count[s:s + 1]
            lag = lag.astype(BF).astype(F32)
            row = j * per + s
            inside = (lag_id >= bounds_ref[row, 0:1]) & (lag_id < bounds_ref[row, 1:2])
            peak_ref[pl.ds(row, 1), :] = jnp.max(
                jnp.where(inside, lag, -jnp.inf), axis=0, keepdims=True)
            lag_ref[row] = lag.T.astype(BF)
        return 0

    lax.fori_loop(0, group, one, 0, unroll=group <= 2)


def local(n, spectra, valid, sources, bounds):
    _, bins, rows, chans = spectra.shape
    per = sources.shape[0]
    group = n // 4
    count = bounds.shape[0]
    table = jnp.asarray(lag_table(bins, per, L))
    span = per * L + 4 * per
    vmem = pl.BlockSpec(memory_space=pltpu.VMEM)
    hbm = pl.BlockSpec(memory_space=pl.ANY)
    dma = pltpu.SemaphoreType.DMA
    half = n // 2
    total = pl.pallas_call(
        functools.partial(kernel, n),
        out_shape=jax.ShapeDtypeStruct((group, span, chans), F32),
        in_specs=[pl.BlockSpec(memory_space=pltpu.SMEM), hbm, hbm, hbm],
        out_specs=vmem,
        scratch_shapes=[
            pltpu.VMEM((2, bins, rows, chans), BF),
            pltpu.VMEM((rows, chans), jnp.int32),
            pltpu.VMEM(table.shape, BF),
            pltpu.VMEM((bins // CHUNKS * chans, chans), BF),
            pltpu.VMEM((n, bins // 8 * 12 * per, chans), BF),
            pltpu.VMEM((n, 2 * per, chans), F32),
            pltpu.VMEM((2, n, 4 * per, chans), F32),
            pltpu.VMEM((n, 2 * bins * per, chans), BF),
            pltpu.VMEM((n, span, chans), BF),
            pltpu.VMEM((2, group, span, chans), BF),
            pltpu.VMEM((group, span, chans), BF),
            pltpu.VMEM((group, span, chans), BF),
            dma((CHUNKS,)), dma, dma,
            dma((half, CHUNKS + 1)), dma((CHUNKS + 1,)), dma((half, CHUNKS + 1)),
            dma((n, CHUNKS + 1)), dma((3, 2)), dma((3, 2)),
        ],
        compiler_params=pltpu.CompilerParams(
            collective_id=0, has_side_effects=True, vmem_limit_bytes=62 * 1024 * 1024),
    )(sources, spectra, valid, table)
    return pl.pallas_call(
        functools.partial(finish, per),
        out_shape=(jax.ShapeDtypeStruct((count, chans, L), BF),
                   jax.ShapeDtypeStruct((count, chans), F32)),
        in_specs=[vmem, vmem],
        out_specs=(vmem, vmem),
        compiler_params=pltpu.CompilerParams(vmem_limit_bytes=32 * 1024 * 1024),
    )(total, bounds.transpose(0, 2, 1))


def solution(mesh):
    in_specs = (P(None, None, "freq", "rcv"), P(None, "rcv"), P("rcv"), P("freq", "rcv", None))
    out_specs = (P("freq", "rcv", None), P("freq", "rcv"))
    return jax.shard_map(functools.partial(local, mesh.shape["rcv"]), mesh=mesh,
                         in_specs=in_specs, out_specs=out_specs, check_vma=False)
```
